32 devices in a mesh: grp: 4 (over z), shard: 8 (over y, x, core).
Axes of the slice: x: 2, y: 2, z: 4, core: 2. Of those that a mesh axis runs over, the one named last changes fastest.
Arguments:
- context: bfloat16 [16384, 2048], P(('grp', 'shard')), may hold values from -6 to 6
- cotangent: bfloat16 [16384, 2048], P(('grp', 'shard')), may hold values from -0.046875 to 0.046875
- master: float32 [2048, 2048], P('shard'), may hold values from -0.125 to 0.125
- moment_one: float32 [2048, 2048], P('shard'), may hold values from -1.8 to 1.8
- moment_two: float32 [2048, 2048], P('shard'), may hold values from 0.3 to 3
Outputs:
- projected: bfloat16 [16384, 2048], P(('grp', 'shard'))
- context_grad: bfloat16 [16384, 2048], P(('grp', 'shard'))
- master_new: float32 [2048, 2048], P('shard')
- moment_one_new: float32 [2048, 2048], P('shard')
- moment_two_new: float32 [2048, 2048], P('shard')
The draws below stay inside these ranges and needn't reach their ends.
All inputs are finite; a program needn't handle non-finite values.
Results may differ from the reference program's by a relative error of at most 0.0065.
Values may be sent and summed in bfloat16 or wider, within the bound.
No kernel may reach another device: no remote copies, remote signals or barrier semaphores. Data moves between devices by JAX's collectives and lax.ppermute only.
A program may use at most 128 MiB of HBM per device.

```python
import math
import jax
import jax.numpy as jnp
from jax import lax

D = 2048
TOKENS = 16384


def spiked(array, own_key, source, target, blocks, factor):
    def block_of(position):
        return (jnp.arange(array.shape[position]) // (array.shape[position] // blocks)).reshape((-1,) + (1,) * (array.ndim - 1 - position))

    first = jax.random.permutation(own_key, blocks)[block_of(target)]
    far = (block_of(target) + blocks // 2) % blocks
    return jnp.where((block_of(source) == first) | (block_of(source) == far), factor * array, array)


def shard_levels(key, dims, cuts, low, top_value):
    level, own = 1.0, jax.random.fold_in(key, 6)
    for axis_at, parts in cuts:
        heights = jnp.exp(jax.random.uniform(jax.random.fold_in(own, axis_at), (parts,), jnp.float32, low / len(cuts), top_value / len(cuts)))
        level = level * jnp.repeat(heights, dims[axis_at] // parts).reshape([-1 if axis == axis_at else 1 for axis in range(len(dims))])
    return level


def normal_values(key, shape, width, bound, pieces=(), kind=jnp.bfloat16):
    result = width * jax.random.normal(key, shape, jnp.float32)
    if pieces:
        result = result * shard_levels(key, shape, pieces, -0.22, 0.18)
    return jnp.clip(result, -bound, bound).astype(kind)


def heavy_noise(key, dims, scale, bound, shards, heavy, dtype=jnp.bfloat16):
    values = scale * jax.random.normal(key, dims, jnp.float32)
    if shards:
        values = values * shard_levels(key, dims, shards, -0.22, 0.18)
    return jnp.clip(spiked(values, jax.random.fold_in(key, 3), *heavy), -bound, bound).astype(dtype)


def setup_inputs(seed: int = 0) -> dict:
    streams_of = jax.random.split(jax.random.key(seed), 6)
    return {
        "context": heavy_noise(streams_of[0], (TOKENS, D), 1.0, 6.0, ((0, 32),), (0, 1, 32, 2.75)),
        "cotangent": normal_values(streams_of[1], (TOKENS, D), (1.0 / TOKENS ** 0.5), 0.046875, ((0, 32),)),
        "master": normal_values(streams_of[2], (D, D), D ** -0.5, 0.125, ((0, 8),), jnp.float32),
        "moment_one": normal_values(streams_of[3], (D, D), 0.3, 1.8, ((0, 8),), jnp.float32),
        "moment_two": jnp.clip(jnp.exp(math.log(3.0) - 2.3025851 * jax.random.uniform(streams_of[4], (D, D), jnp.float32) ** shard_levels(streams_of[4], (D, D), ((0, 8),), -0.2, 0.2)), 0.3, 3.0),
    }


first_fix = 0.99997343860111
second_fix = 0.99407947078

def adamw(master, moment_one, moment_two, grad):
    one_new = 0.9 * moment_one + 0.1 * grad
    two_new = 0.95 * moment_two + 0.05 * grad * grad
    update = one_new / first_fix / (jnp.sqrt(two_new / second_fix) + 1e-08)
    master_new = master - 0.01 * (update + 0.1 * master)
    return (master_new, one_new, two_new)

def reference(context, cotangent, master, moment_one, moment_two):
    weights = master.astype(jnp.bfloat16)
    projected = jnp.dot(context, weights, preferred_element_type=jnp.float32).astype(jnp.bfloat16)
    context_grad = lax.dot_general(cotangent, weights, (((1,), (1,)), ((), ())), preferred_element_type=jnp.float32).astype(jnp.bfloat16)
    grad = lax.dot_general(context, cotangent, (((0,), (0,)), ((), ())), preferred_element_type=jnp.float32)
    master_new, one_new, two_new = adamw(master, moment_one, moment_two, grad)
    return (projected, context_grad, master_new, one_new, two_new)
```

```python
import jax
import jax.numpy as jnp
from jax import lax
from jax.experimental import pallas as pl
from jax.experimental.pallas import tpu as pltpu
from jax.sharding import PartitionSpec as P

first_fix = 0.99997343860111
second_fix = 0.99407947078
CHUNKS = (2, 1, 1)


def adamw(master, moment_one, moment_two, grad):
    one_new = 0.9 * moment_one + 0.1 * grad
    two_new = 0.95 * moment_two + 0.05 * grad * grad
    update = one_new / first_fix / (jnp.sqrt(two_new / second_fix) + 1e-08)
    master_new = master - 0.01 * (update + 0.1 * master)
    return (master_new, one_new, two_new)


def plain_body(context, cotangent, master, moment_one, moment_two):
    weights = lax.all_gather(master.astype(jnp.bfloat16), "shard", axis=0, tiled=True)
    projected = jnp.dot(context, weights, preferred_element_type=jnp.float32).astype(jnp.bfloat16)
    context_grad = lax.dot_general(
        cotangent, weights, (((1,), (1,)), ((), ())), preferred_element_type=jnp.float32
    ).astype(jnp.bfloat16)
    partial_grad = lax.psum_scatter(
        lax.dot_general(
            context, cotangent, (((0,), (0,)), ((), ())), preferred_element_type=jnp.float32
        ).astype(jnp.bfloat16),
        "shard",
        scatter_dimension=0,
        tiled=True,
    )
    grad = lax.psum(partial_grad, "grp").astype(jnp.float32)
    return (projected, context_grad, *adamw(master, moment_one, moment_two, grad))


ANY = pl.BlockSpec(memory_space=pl.ANY)
SMEM = pl.BlockSpec(memory_space=pltpu.SMEM)
VMEM = pl.BlockSpec(memory_space=pltpu.VMEM)


def dot(a, b, contract=(1, 0)):
    return lax.dot_general(a, b, (((contract[0],), (contract[1],)), ((), ())), preferred_element_type=jnp.float32)


def after(array, *others):
    return lax.optimization_barrier((array, *others))[0]


def add(a, b):
    return (a.astype(jnp.float32) + b.astype(jnp.float32)).astype(jnp.bfloat16)


def call(kernel, name, flops, outs, in_specs, out_specs, scratch=(), aliases=None):
    return pl.pallas_call(
        kernel,
        out_shape=outs,
        in_specs=in_specs,
        out_specs=out_specs,
        scratch_shapes=list(scratch),
        input_output_aliases=aliases or {},
        compiler_params=pltpu.CompilerParams(vmem_limit_bytes=56 * 2**20),
        cost_estimate=pl.CostEstimate(flops=flops, bytes_accessed=0, transcendentals=0),
        name=name,
    )


def aligned(index, rows):
    return pl.ds(pl.multiple_of(index * rows, rows), rows)


def grad_blocks(info, parts, contexts, cotangents, rows, subs):
    tokens, width = cotangents[0].shape
    half = width // 2
    sizes = [half * units // sum(CHUNKS) for units in CHUNKS]
    starts = [sum(sizes[:k]) for k in range(len(sizes))]
    count = len(parts[0])
    order = sorted({r for part in parts for r in part}, key=lambda r: -sum(r in part for part in parts))
    step = rows // subs

    def spans(r):
        wanted = [h for h in range(2) if r in parts[h]]
        return wanted[0] * half, (wanted[-1] + 1) * half

    def fill(info_ref, c0, c1, t0, t1, *out_refs):
        for r in order:
            at = aligned(info_ref[0] ^ r, rows)
            lo, hi = spans(r)
            total = dot(c0[:, at], t0[:, lo:hi], (0, 0)) + dot(c1[:, at], t1[:, lo:hi], (0, 0))
            total = total.astype(jnp.bfloat16)
            for h in range(2):
                if r in parts[h]:
                    for k, size in enumerate(sizes):
                        start = h * half + starts[k] - lo
                        for j in range(subs):
                            place = pl.multiple_of(parts[h].index(r) * rows + (info_ref[1] ^ j) * step, step)
                            out_refs[2 * k + h][pl.ds(place, step), :] = total[j * step : (j + 1) * step, start : start + size]

    def plain(h, k):
        cols = slice(h * half + starts[k], h * half + starts[k] + sizes[k])
        result = []
        for r in parts[h]:
            total = sum(
                dot(lax.dynamic_slice_in_dim(c, (info[0] ^ r) * rows, rows, axis=1), t[:, cols], (0, 0))
                for c, t in zip(contexts, cotangents)
            )
            result.append(reordered(total.astype(jnp.bfloat16), info[1], subs))
        return jnp.concatenate(result, axis=0)

    if rows % 128 or step % 16:
        return [[plain(h, k) for h in range(2)] for k in range(len(sizes))]
    outs = tuple(jax.ShapeDtypeStruct((count * rows, size), jnp.bfloat16) for size in sizes for _ in range(2))
    flops = 4 * count * rows * width * tokens
    result = call(fill, "grad_blocks", flops, outs, [SMEM] + [VMEM] * 4, (VMEM,) * len(outs))(info, *contexts, *cotangents)
    return [[result[2 * k + h] for h in range(2)] for k in range(len(sizes))]


def reordered(array, low, subs):
    step = array.shape[0] // subs
    return jnp.concatenate(
        [lax.dynamic_slice_in_dim(array, (low ^ j) * step, step, axis=0) for j in range(subs)], axis=0
    )


def sources(pieces):
    arrays = []
    for piece in pieces:
        if not any(piece[2] is array for array in arrays):
            arrays.append(piece[2])
    return arrays, [[piece[2] is array for array in arrays].index(True) for piece in pieces]


def run(copies):
    for copy in copies:
        copy.start()
    for copy in copies:
        copy.wait()


def weight_copies(info_ref, pieces, index, refs, blocks, weights, rows):
    width = weights.shape[1]
    copies = []
    for (r, half, _, row), source in zip(pieces, index):
        at = pl.ds(blocks.index(r) * rows, rows)
        target = weights.at[at, :]
        if half is not None:
            lo = pl.multiple_of((lax.rem(info_ref[1], 2) ^ half) * (width // 2), width // 2)
            target = weights.at[at, pl.ds(lo, width // 2)]
        copies.append((refs[source].at[pl.ds(row, rows), :], target))
    return copies


def products(info, pieces, context, cotangent, rows, kind):
    tokens, width = context.shape
    blocks = sorted({piece[0] for piece in pieces})
    depth = len(blocks) * rows
    arrays, index = sources(pieces)
    tile = min(512, width)

    def kernel(info_ref, context_ref, cotangent_ref, *rest):
        refs = rest[: len(arrays)]
        product_ref, columns_ref, weights, chosen, in_sems = rest[len(arrays) :]
        copies = weight_copies(info_ref, pieces, index, refs, blocks, weights, rows)
        for i, r in enumerate(blocks):
            copies.append((context_ref.at[:, aligned(info_ref[0] ^ r, rows)], chosen.at[:, pl.ds(i * rows, rows)]))
        run([pltpu.make_async_copy(a, b, in_sems.at[i]) for i, (a, b) in enumerate(copies)])
        columns_ref[...] = dot(cotangent_ref[...], weights[...], (1, 1)).astype(jnp.bfloat16)
        for i in range(width // tile):
            at = pl.ds(i * tile, tile)
            product_ref[:, at] = dot(chosen[...], weights[:, at]).astype(kind)

    scratch = [
        pltpu.VMEM((depth, width), jnp.bfloat16),
        pltpu.VMEM((tokens, depth), jnp.bfloat16),
        pltpu.SemaphoreType.DMA((len(pieces) + len(blocks),)),
    ]
    return call(
        kernel,
        "products",
        4 * tokens * depth * width,
        (jax.ShapeDtypeStruct((tokens, width), kind), jax.ShapeDtypeStruct((tokens, depth), jnp.bfloat16)),
        [SMEM, ANY, VMEM] + [ANY] * len(arrays),
        (VMEM, VMEM),
        scratch,
    )(info, context, cotangent, *arrays)


def joined(info, own, got, own_columns, got_columns, blocks, rows):
    tokens, width = own.shape
    placed = [(r ^ core, core, i) for core in range(2) for i, r in enumerate(blocks)]

    def kernel(info_ref, own_ref, got_ref, own_columns_ref, got_columns_ref, product_ref, out_ref, sems):
        refs = (own_columns_ref, got_columns_ref)
        copies = [
            pltpu.make_async_copy(
                refs[n].at[:, pl.ds(i * rows, rows)], out_ref.at[:, aligned(info_ref[0] ^ r, rows)], sems.at[place]
            )
            for place, (r, n, i) in enumerate(placed)
        ]
        for copy in copies:
            copy.start()
        product_ref[...] = (own_ref[...] + got_ref[...].astype(jnp.float32)).astype(jnp.bfloat16)
        for copy in copies:
            copy.wait()

    out = jax.ShapeDtypeStruct((tokens, width), jnp.bfloat16)
    return call(
        kernel,
        "joined",
        tokens * width,
        (out, out),
        [SMEM] + [VMEM] * 4,
        (VMEM, ANY),
        [pltpu.SemaphoreType.DMA((len(placed),))],
    )(info, own, got, own_columns, got_columns)


def plain_products(info, pieces, context, cotangent, rows):
    width = context.shape[1]
    weights = jnp.zeros((width, width), jnp.bfloat16)
    for r, half, array, row in pieces:
        lo = 0 if half is None else (lax.rem(info[1], 2) ^ half) * (width // 2)
        weights = lax.dynamic_update_slice(weights, array[row : row + rows], ((info[0] ^ r) * rows, lo))
    return dot(context, weights).astype(jnp.bfloat16), dot(cotangent, weights, (1, 1)).astype(jnp.bfloat16)


def make_body(groups, shards):
    bits = shards.bit_length() - 1
    x_masks = [2 << i for i in range((bits - 1) // 2)]
    y_masks = [2 << i for i in range((bits - 1) // 2, bits - 1)]
    masks = (x_masks + y_masks, y_masks + x_masks)
    subs = groups // 2
    group_masks = [1 << i for i in reversed(range(subs.bit_length() - 1))]

    def swap(array, mask):
        return lax.ppermute(array, "shard", [(i, i ^ mask) for i in range(shards)])

    def swap_group(array, mask):
        return lax.ppermute(array, "grp", [(i, i ^ mask) for i in range(groups)])

    def spread(pieces, masks):
        for mask in masks:
            pieces = {**pieces, **{r ^ mask: swap(piece, mask) for r, piece in pieces.items()}}
        return pieces

    def halving(masks):
        blocks = [0]
        for mask in reversed(masks):
            blocks = blocks + [b ^ mask for b in blocks]
        return blocks

    def body(context, cotangent, master, moment_one, moment_two):
        shard, group = lax.axis_index("shard"), lax.axis_index("grp")
        rows, width = master.shape
        half = width // 2
        odd = lax.rem(group, 2)
        low = lax.rem(group, subs)
        info = jnp.stack([shard, low if subs > 1 else odd])
        order_of_rows = low
        tiled = rows % 128 == 0 and (rows // subs) % 16 == 0 and subs > 1
        latest = []

        def then(array):
            return after(array, *latest)

        def did(result):
            latest[:] = [result]
            return result

        def named(names, array, flip=0):
            return [(r, h ^ flip, array, i * rows) for i, (r, h) in enumerate(names)]

        contexts, cotangents = (context, swap(context, 1)), (cotangent, swap(cotangent, 1))

        weights = master.astype(jnp.bfloat16)
        left, right = weights[:, :half], weights[:, half:]
        mine, other = jnp.where(odd == 1, right, left), jnp.where(odd == 1, left, right)
        near_x = {r: p for r, p in spread({0: mine}, x_masks).items() if r}
        near_y = {r: p for r, p in spread({0: other}, y_masks).items() if r}

        orders = [halving(m) for m in masks]
        count = len(orders[0]) // 2
        sent = grad_blocks(info, [o[count:] for o in orders], contexts, cotangents, rows, subs)
        did(sent[-1][-1])
        got = {0: [swap(sent[0][h], masks[h][0]) for h in range(2)]}

        near = jnp.concatenate([then(p) for p in [*near_x.values(), *near_y.values()]], axis=0)
        did(near)
        near_names = [(r, 0) for r in near_x] + [(r, 1) for r in near_y]
        near_group = swap_group(near, 1)
        far_x = spread({r: then(p) for r, p in near_x.items()}, y_masks)
        far_y = spread({r: then(p) for r, p in near_y.items()}, x_masks)
        far_names = [(r, 0) for r in far_x if r not in near_x] + [(r, 1) for r in far_y if r not in near_y]
        far = [(far_x, far_y)[h][r] for r, h in far_names]
        pieces = [(0, None, weights, 0)] + named(near_names, near) + named(near_names, near_group, flip=1)
        pieces += [(r, h, array, 0) for (r, h), array in zip(far_names, far)]
        kept = grad_blocks(info, [o[:count] for o in orders], contexts, (then(cotangent), cotangents[1]), rows, subs)
        did(kept[-1][-1])

        def halve_all(k, level):
            come, got[k] = got[k], [None, None]
            for h in range(2):
                total = did(add(kept[k][h], then(come[h])))
                size = total.shape[0] // 2
                kept[k][h], got[k][h] = total[:size], swap(total[size:], masks[h][level])

        summed, come, stage = {}, {}, {}

        def enter(k):
            parts = [did(add(kept[k][h], then(got[k][h]))) for h in range(2)]
            summed[k], stage[k] = jnp.concatenate(parts, axis=1), 0
            leave(k)

        def leave(k):
            j, steps = stage[k], len(group_masks)
            if j < steps:
                size = summed[k].shape[0] // 2
                come[k] = swap_group(summed[k][size:], group_masks[j])
                summed[k] = summed[k][:size]
            elif j == steps:
                come[k] = swap_group(summed[k], subs)
            elif j <= 2 * steps:
                come[k] = swap_group(summed[k], group_masks[2 * steps - j])

        def advance(k):
            if stage[k] <= len(group_masks):
                summed[k] = did(add(summed[k], then(come[k])))
            else:
                summed[k] = did(jnp.concatenate([summed[k], then(come[k])], axis=0))
            stage[k] += 1
            leave(k)

        last = 2 * len(group_masks) + 1
        levels = len(masks[0])
        chunks = len(CHUNKS)

        def halve_to_end(k, start):
            for level in range(start, levels):
                halve_all(k, level)

        def begin(k, *also):
            got[k] = [swap(after(sent[k][h], *latest, *also), masks[h][0]) for h in range(2)]

        halve_to_end(0, 1)
        begin(1, *far)
        enter(0)
        if tiled:
            blocks = sorted({piece[0] for piece in pieces})
            sent_part, sent_columns = products(info, pieces, then(contexts[1]), cotangents[1], rows, jnp.bfloat16)
            did(sent_part)
            got_part, got_columns = swap(sent_part, 1), swap(sent_columns, 1)
        halve_to_end(1, 1)
        begin(2)
        advance(0)
        enter(1)
        if tiled:
            part, own_columns = products(info, pieces, then(context), cotangent, rows, jnp.float32)
            did(part)
        halve_to_end(2, 1)
        advance(0)
        enter(2)
        advance(1)
        if tiled:
            projected, columns = joined(info, then(part), got_part, own_columns, got_columns, blocks, rows)
            did(projected)
        else:
            pieces += [(r ^ 1, h, swap(array, 1), row) for r, h, array, row in pieces]
            projected, columns = plain_products(info, pieces, context, cotangent, rows)
        advance(2)
        advance(1)
        while any(stage[k] < last for k in range(chunks)):
            for k in range(chunks):
                if stage[k] < last:
                    advance(k)
        sizes = [half * units // sum(CHUNKS) for units in CHUNKS]
        grad = [summed[k][:, h * sizes[k] : (h + 1) * sizes[k]] for h in range(2) for k in range(chunks)]
        grad = reordered(jnp.concatenate(grad, axis=1), order_of_rows, subs).astype(jnp.float32)
        updated = adamw(master, moment_one, moment_two, grad)
        return (projected, columns, *updated)

    return body


def power_of_two(n):
    return n > 0 and n & (n - 1) == 0


def solution(mesh):
    groups, shards = mesh.shape["grp"], mesh.shape["shard"]
    regular = power_of_two(groups) and power_of_two(shards) and groups >= 2 and shards >= 8
    token, state = P(("grp", "shard"), None), P("shard", None)
    return jax.shard_map(
        make_body(groups, shards) if regular else plain_body,
        mesh=mesh,
        in_specs=(token, token, state, state, state),
        out_specs=(token, token, state, state, state),
        check_vma=False,
    )
```

```python
import jax
import jax.numpy as jnp
from jax import lax
from jax.experimental import pallas as pl
from jax.experimental.pallas import tpu as pltpu
from jax.sharding import PartitionSpec as P

first_fix = 0.99997343860111
second_fix = 0.99407947078
CHUNKS = (5, 3)


def adamw(master, moment_one, moment_two, grad):
    one_new = 0.9 * moment_one + 0.1 * grad
    two_new = 0.95 * moment_two + 0.05 * grad * grad
    update = one_new / first_fix / (jnp.sqrt(two_new / second_fix) + 1e-08)
    master_new = master - 0.01 * (update + 0.1 * master)
    return (master_new, one_new, two_new)


def plain_body(context, cotangent, master, moment_one, moment_two):
    weights = lax.all_gather(master.astype(jnp.bfloat16), "shard", axis=0, tiled=True)
    projected = jnp.dot(context, weights, preferred_element_type=jnp.float32).astype(jnp.bfloat16)
    context_grad = lax.dot_general(
        cotangent, weights, (((1,), (1,)), ((), ())), preferred_element_type=jnp.float32
    ).astype(jnp.bfloat16)
    partial_grad = lax.psum_scatter(
        lax.dot_general(
            context, cotangent, (((0,), (0,)), ((), ())), preferred_element_type=jnp.float32
        ).astype(jnp.bfloat16),
        "shard",
        scatter_dimension=0,
        tiled=True,
    )
    grad = lax.psum(partial_grad, "grp").astype(jnp.float32)
    return (projected, context_grad, *adamw(master, moment_one, moment_two, grad))


ANY = pl.BlockSpec(memory_space=pl.ANY)
SMEM = pl.BlockSpec(memory_space=pltpu.SMEM)
VMEM = pl.BlockSpec(memory_space=pltpu.VMEM)


def dot(a, b, contract=(1, 0)):
    return lax.dot_general(a, b, (((contract[0],), (contract[1],)), ((), ())), preferred_element_type=jnp.float32)


def after(array, *others):
    return lax.optimization_barrier((array, *others))[0]


def add(a, b):
    return (a.astype(jnp.float32) + b.astype(jnp.float32)).astype(jnp.bfloat16)


def call(kernel, name, flops, outs, in_specs, out_specs, scratch=(), aliases=None):
    return pl.pallas_call(
        kernel,
        out_shape=outs,
        in_specs=in_specs,
        out_specs=out_specs,
        scratch_shapes=list(scratch),
        input_output_aliases=aliases or {},
        compiler_params=pltpu.CompilerParams(vmem_limit_bytes=24 * 2**20),
        cost_estimate=pl.CostEstimate(flops=16 * flops, bytes_accessed=0, transcendentals=0),
        name=name,
    )


def aligned(index, rows):
    return pl.ds(pl.multiple_of(index * rows, rows), rows)


def grad_blocks(info, parts, contexts, cotangents, rows, subs):
    tokens, width = cotangents[0].shape
    half = width // 2
    sizes = [half * units // sum(CHUNKS) for units in CHUNKS]
    starts = [sum(sizes[:k]) for k in range(len(sizes))]
    count = len(parts[0])
    order = sorted({r for part in parts for r in part}, key=lambda r: -sum(r in part for part in parts))
    step = rows // subs

    def spans(r):
        wanted = [h for h in range(2) if r in parts[h]]
        return wanted[0] * half, (wanted[-1] + 1) * half

    def fill(info_ref, c0, c1, t0, t1, *out_refs):
        for r in order:
            at = aligned(info_ref[0] ^ r, rows)
            lo, hi = spans(r)
            total = dot(c0[:, at], t0[:, lo:hi], (0, 0)) + dot(c1[:, at], t1[:, lo:hi], (0, 0))
            total = total.astype(jnp.bfloat16)
            for h in range(2):
                if r in parts[h]:
                    for k, size in enumerate(sizes):
                        start = h * half + starts[k] - lo
                        for j in range(subs):
                            place = pl.multiple_of(parts[h].index(r) * rows + (info_ref[1] ^ j) * step, step)
                            out_refs[2 * k + h][pl.ds(place, step), :] = total[j * step : (j + 1) * step, start : start + size]

    def plain(h, k):
        cols = slice(h * half + starts[k], h * half + starts[k] + sizes[k])
        result = []
        for r in parts[h]:
            total = sum(
                dot(lax.dynamic_slice_in_dim(c, (info[0] ^ r) * rows, rows, axis=1), t[:, cols], (0, 0))
                for c, t in zip(contexts, cotangents)
            )
            result.append(reordered(total.astype(jnp.bfloat16), info[1], subs))
        return jnp.concatenate(result, axis=0)

    if rows % 128 or step % 16:
        return [[plain(h, k) for h in range(2)] for k in range(len(sizes))]
    outs = tuple(jax.ShapeDtypeStruct((count * rows, size), jnp.bfloat16) for size in sizes for _ in range(2))
    flops = 4 * count * rows * width * tokens
    result = call(fill, "grad_blocks", flops, outs, [SMEM] + [VMEM] * 4, (VMEM,) * len(outs))(info, *contexts, *cotangents)
    return [[result[2 * k + h] for h in range(2)] for k in range(len(sizes))]


def reordered(array, low, subs):
    step = array.shape[0] // subs
    return jnp.concatenate(
        [lax.dynamic_slice_in_dim(array, (low ^ j) * step, step, axis=0) for j in range(subs)], axis=0
    )


def sources(pieces):
    arrays = []
    for piece in pieces:
        if not any(piece[2] is array for array in arrays):
            arrays.append(piece[2])
    return arrays, [[piece[2] is array for array in arrays].index(True) for piece in pieces]


def started(pairs, sems, first=0):
    copies = [pltpu.make_async_copy(a, b, sems.at[first + i]) for i, (a, b) in enumerate(pairs)]
    for copy in copies:
        copy.start()
    return copies


def wait(copies):
    for copy in copies:
        copy.wait()


def weight_copies(info_ref, pieces, index, refs, blocks, weights, rows, half):
    size = weights.shape[1] // 2
    lo = pl.multiple_of((lax.rem(info_ref[1], 2) ^ half) * size, size)
    copies = {}
    for (r, which, _, row), source in zip(pieces, index):
        if which in (None, half):
            origin = refs[source].at[pl.ds(row, rows), :]
            if which is None:
                origin = refs[source].at[pl.ds(row, rows), pl.ds(lo, size)]
            copies[r] = (origin, weights.at[pl.ds(blocks.index(r) * rows, rows), pl.ds(half * size, size)])
    return copies


def product(info, pieces, context, rows, got=None):
    tokens, width = context.shape
    half = width // 2
    blocks = sorted({piece[0] for piece in pieces})
    depth = len(blocks) * rows
    arrays, index = sources(pieces)
    more = [] if got is None else [got]
    tile = min(512, half)
    tiles = half // tile
    reads = len(blocks)

    def kernel(info_ref, context_ref, *rest):
        refs = rest[: len(arrays)]
        got_refs = rest[len(arrays) : len(arrays) + len(more)]
        out_ref, weights, chosen, result, in_sems, out_sems, *held = rest[len(arrays) + len(more) :]
        columns = [
            (context_ref.at[:, aligned(info_ref[0] ^ r, rows)], chosen.at[:, pl.ds(i * rows, rows)])
            for i, r in enumerate(blocks)
        ]
        inward = [started(columns, in_sems)]
        for side in range(2):
            pairs = weight_copies(info_ref, pieces, index, refs, blocks, weights, rows, side)
            inward.append(started([pairs[r] for r in blocks], in_sems, reads * (1 + side)))
        adding = started(list(zip(got_refs, held)), in_sems, 3 * reads)
        wait(inward[0])
        outward = []
        for side in range(2):
            wait(inward[1 + side])
            lo = (lax.rem(info_ref[1], 2) ^ side) * half
            for i in range(tiles):
                part = dot(chosen[...], weights[:, pl.ds(side * half + i * tile, tile)])
                at = pl.ds(pl.multiple_of(lo + i * tile, tile), tile)
                if more:
                    wait(adding)
                    adding = []
                    part = part + held[0][:, at].astype(jnp.float32)
                place = side * tiles + i
                result[:, pl.ds(place * tile, tile)] = part.astype(jnp.bfloat16)
                outward += started([(result.at[:, pl.ds(place * tile, tile)], out_ref.at[:, at])], out_sems, place)
        wait(outward)

    return call(
        kernel,
        "product",
        2 * tokens * depth * width,
        jax.ShapeDtypeStruct((tokens, width), jnp.bfloat16),
        [SMEM, ANY] + [ANY] * (len(arrays) + len(more)),
        ANY,
        [
            pltpu.VMEM((depth, width), jnp.bfloat16),
            pltpu.VMEM((tokens, depth), jnp.bfloat16),
            pltpu.VMEM((tokens, width), jnp.bfloat16),
            pltpu.SemaphoreType.DMA((3 * reads + 1,)),
            pltpu.SemaphoreType.DMA((2 * tiles,)),
        ]
        + [pltpu.VMEM((tokens, width), jnp.bfloat16)] * len(more),
    )(info, context, *arrays, *more)


def grad_columns(info, pieces, cotangent, rows, got=None):
    tokens, width = cotangent.shape
    half = width // 2
    blocks = sorted({piece[0] for piece in pieces})
    depth = len(blocks) * rows
    arrays, index = sources(pieces)
    more = [] if got is None else [got]
    reads = len(blocks)
    group = max(1, reads // 2)

    def kernel(info_ref, cotangent_ref, *rest):
        refs = rest[: len(arrays)]
        got_refs = rest[len(arrays) : len(arrays) + len(more)]
        out_ref, weights, turned, result, in_sems, out_sems, *held = rest[len(arrays) + len(more) :]
        halves = []
        for side in range(2):
            lo = pl.multiple_of((lax.rem(info_ref[1], 2) ^ side) * half, half)
            halves.append((cotangent_ref.at[:, pl.ds(lo, half)], turned.at[:, pl.ds(side * half, half)]))
        first = started(halves, in_sems, 2 * reads)
        pairs = [weight_copies(info_ref, pieces, index, refs, blocks, weights, rows, side) for side in range(2)]
        inward = [started([pairs[side][r] for side in range(2)], in_sems, 2 * i) for i, r in enumerate(blocks)]
        placing = started(list(zip(got_refs, held)), in_sems, 2 * reads + 2)
        outward = []
        wait(first)
        for start in range(0, reads, group):
            for i in range(start, start + group):
                wait(inward[i])
            at = pl.ds(start * rows, group * rows)
            result[:, at] = dot(turned[...], weights[at, :], (1, 1)).astype(jnp.bfloat16)
            for i in range(start, start + group):
                at = pl.ds(i * rows, rows)
                target = out_ref.at[:, aligned(info_ref[0] ^ blocks[i], rows) if more else at]
                outward += started([(result.at[:, at], target)], out_sems, i)
            if placing:
                wait(placing)
                placing = []
                for i, r in enumerate(blocks):
                    target = out_ref.at[:, aligned(info_ref[0] ^ r ^ 1, rows)]
                    outward += started([(held[0].at[:, pl.ds(i * rows, rows)], target)], out_sems, reads + i)
        wait(outward)

    return call(
        kernel,
        "grad_columns",
        2 * tokens * depth * width,
        jax.ShapeDtypeStruct((tokens, width if more else depth), jnp.bfloat16),
        [SMEM, ANY] + [ANY] * (len(arrays) + len(more)),
        ANY,
        [
            pltpu.VMEM((depth, width), jnp.bfloat16),
            pltpu.VMEM((tokens, width), jnp.bfloat16),
            pltpu.VMEM((tokens, depth), jnp.bfloat16),
            pltpu.SemaphoreType.DMA((2 * reads + 3,)),
            pltpu.SemaphoreType.DMA((2 * reads,)),
        ]
        + [pltpu.VMEM((tokens, depth), jnp.bfloat16)] * len(more),
    )(info, cotangent, *arrays, *more)


def stepped(info, side, pieces, state, so_far=None):
    rows, width = state[0].shape
    lines = rows // 2
    arrays = []
    for piece in pieces:
        if not any(piece[0] is array for array in arrays):
            arrays.append(piece[0])
    more = [] if so_far is None else list(so_far)

    def kernel(info_ref, *rest):
        grads, rest = rest[: len(arrays)], rest[len(arrays) :]
        states, rest = rest[:3], rest[3 + len(more) :]
        outs, held, results, in_sems, out_sems = rest[:3], rest[3:6], rest[6:9], rest[9], rest[10]
        at = aligned(info_ref[1] ^ side, lines)
        inward, outward = [], []
        for n, (_, _, to, size) in enumerate(pieces):
            cols = pl.ds(to, size)
            inward.append(started([(states[i].at[at, cols], held[i].at[:, cols]) for i in range(3)], in_sems, 3 * n))
        for n, (array, start, to, size) in enumerate(pieces):
            wait(inward[n])
            cols = pl.ds(to, size)
            grad_ref = grads[[array is other for other in arrays].index(True)]
            grad = grad_ref[:, pl.ds(start, size)].astype(jnp.float32)
            values = adamw(held[0][:, cols], held[1][:, cols], held[2][:, cols], grad)
            for result, value in zip(results, values):
                result[:, cols] = value
            outward += started([(results[i].at[:, cols], outs[i].at[at, cols]) for i in range(3)], out_sems, 3 * n)
        wait(outward)

    out = jax.ShapeDtypeStruct((rows, width), jnp.float32)
    first = 4 + len(arrays)
    return call(
        kernel,
        "stepped",
        16 * lines * width,
        (out,) * 3,
        [SMEM] + [VMEM] * len(arrays) + [ANY] * (3 + len(more)),
        (ANY,) * 3,
        [pltpu.VMEM((lines, width), jnp.float32)] * 6 + [pltpu.SemaphoreType.DMA((3 * len(pieces),))] * 2,
        {first + i: i for i in range(3)} if more else {},
    )(info, *arrays, *state, *more)


def plain_products(info, pieces, context, cotangent, rows):
    width = context.shape[1]
    weights = jnp.zeros((width, width), jnp.bfloat16)
    for r, half, array, row in pieces:
        lo = 0 if half is None else (lax.rem(info[1], 2) ^ half) * (width // 2)
        weights = lax.dynamic_update_slice(weights, array[row : row + rows], ((info[0] ^ r) * rows, lo))
    return dot(context, weights).astype(jnp.bfloat16), dot(cotangent, weights, (1, 1)).astype(jnp.bfloat16)


def make_body(groups, shards):
    bits = shards.bit_length() - 1
    x_masks = [2 << i for i in range((bits - 1) // 2)]
    y_masks = [2 << i for i in range((bits - 1) // 2, bits - 1)]
    masks = (x_masks + y_masks, y_masks + x_masks)
    subs = groups // 2
    group_masks = [1 << i for i in reversed(range(subs.bit_length() - 1))]

    def swap(array, mask):
        return lax.ppermute(array, "shard", [(i, i ^ mask) for i in range(shards)])

    def swap_group(array, mask):
        return lax.ppermute(array, "grp", [(i, i ^ mask) for i in range(groups)])

    def spread(pieces, masks):
        for mask in masks:
            pieces = {**pieces, **{r ^ mask: swap(piece, mask) for r, piece in pieces.items()}}
        return pieces

    def halving(masks):
        blocks = [0]
        for mask in reversed(masks):
            blocks = blocks + [b ^ mask for b in blocks]
        return blocks

    def body(context, cotangent, master, moment_one, moment_two):
        shard, group = lax.axis_index("shard"), lax.axis_index("grp")
        rows, width = master.shape
        half = width // 2
        odd = lax.rem(group, 2)
        low = lax.rem(group, subs)
        info = jnp.stack([shard, low if subs > 1 else odd])
        order_of_rows = low
        tiled = rows % 128 == 0 and subs == 2
        latest = []

        def then(array):
            return after(array, *latest)

        def did(result):
            latest[:] = [result]
            return result

        def named(names, array, flip=0):
            return [(r, h ^ flip, array, i * rows) for i, (r, h) in enumerate(names)]

        contexts, cotangents = (context, swap(context, 1)), (cotangent, swap(cotangent, 1))

        left, right = master[:, :half], master[:, half:]
        mine, other = jnp.where(odd == 1, right, left), jnp.where(odd == 1, left, right)
        mine, other = mine.astype(jnp.bfloat16), other.astype(jnp.bfloat16)
        near_x = {r: p for r, p in spread({0: mine}, x_masks).items() if r}
        near_y = {r: p for r, p in spread({0: other}, y_masks).items() if r}

        orders = [halving(m) for m in masks]
        count = len(orders[0]) // 2
        sent = grad_blocks(info, [o[count:] for o in orders], contexts, cotangents, rows, subs)
        did(sent[-1][-1])
        got = {0: [swap(sent[0][h], masks[h][0]) for h in range(2)]}

        kept = grad_blocks(info, [o[:count] for o in orders], contexts, (then(cotangent), cotangents[1]), rows, subs)
        did(kept[-1][-1])

        far_x = spread({r: then(p) for r, p in near_x.items()}, y_masks)
        far_y = spread({r: then(p) for r, p in near_y.items()}, x_masks)
        far_names = [(r, 0) for r in far_x if r not in near_x] + [(r, 1) for r in far_y if r not in near_y]
        far = [(far_x, far_y)[h][r] for r, h in far_names]
        near = jnp.concatenate([then(p) for p in [*near_x.values(), *near_y.values()]], axis=0)
        near_names = [(r, 0) for r in near_x] + [(r, 1) for r in near_y]
        near_group = swap_group(near, 1)
        weights = then(master).astype(jnp.bfloat16)
        pieces = [(0, None, weights, 0)] + named(near_names, near) + named(near_names, near_group, flip=1)
        pieces += [(r, h, array, 0) for (r, h), array in zip(far_names, far)]
        def halve_all(k, level):
            come, got[k] = got[k], [None, None]
            for h in range(2):
                total = did(add(kept[k][h], then(come[h])))
                size = total.shape[0] // 2
                kept[k][h], got[k][h] = total[:size], swap(total[size:], masks[h][level])

        summed, come, stage = {}, {}, {}

        def enter(k, name, halves):
            parts = [did(add(kept[k][h], then(got[k][h]))) for h in halves]
            summed[name], stage[name] = jnp.concatenate(parts, axis=1) if len(parts) > 1 else parts[0], 0
            leave(name)

        def leave(k):
            j, steps = stage[k], len(group_masks)
            if j < steps:
                size = summed[k].shape[0] // 2
                come[k] = swap_group(summed[k][size:], group_masks[j])
                summed[k] = summed[k][:size]
            elif j == steps:
                come[k] = swap_group(summed[k], subs)
            elif j <= 2 * steps:
                come[k] = swap_group(summed[k], group_masks[2 * steps - j])

        def advance(k):
            if stage[k] <= len(group_masks):
                summed[k] = did(add(summed[k], then(come[k])))
            else:
                summed[k] = jnp.concatenate([summed[k], then(come[k])], axis=0)
            stage[k] += 1
            leave(k)

        last = 2 * len(group_masks) + 1
        levels = len(masks[0])

        def halve_to_end(k, start):
            for level in range(start, levels):
                halve_all(k, level)

        def finish(name):
            while stage[name] < last:
                advance(name)

        halve_to_end(0, 1)
        got[1] = [swap(after(sent[1][h], *latest, *far), masks[h][0]) for h in range(2)]
        enter(0, "both", (0, 1))
        if tiled:
            part = did(product(info, pieces, then(contexts[1]), rows))
            got_part = swap(part, 1)
        halve_to_end(1, 1)
        advance("both")
        if tiled:
            columns = did(grad_columns(info, pieces, then(cotangents[1]), rows))
            got_columns = swap(columns, 1)
        enter(1, "first", (0,))
        enter(1, "second", (1,))
        if tiled:
            projected = did(product(info, pieces, then(context), rows, got_part))
        advance("first")
        advance("second")
        advance("both")
        if tiled:
            columns = did(grad_columns(info, pieces, then(cotangent), rows, got_columns))
        else:
            pieces += [(r ^ 1, h, swap(array, 1), row) for r, h, array, row in pieces]
            projected, columns = plain_products(info, pieces, context, cotangent, rows)
        advance("first")
        advance("second")
        if tiled:
            sizes = [half * units // sum(CHUNKS) for units in CHUNKS]

            def columns_of(both, first, second):
                return [
                    (both, 0, 0, sizes[0]),
                    (both, sizes[0], half, sizes[0]),
                    (first, 0, sizes[0], sizes[1]),
                    (second, 0, half + sizes[0], sizes[1]),
                ]

            state = (then(master), moment_one, moment_two)
            state = stepped(info, 0, columns_of(*[summed[name] for name in ("both", "first", "second")]), state)
            grads = columns_of(*[come[name] for name in ("both", "first", "second")])
            state = stepped(info, 1, grads, (master, moment_one, moment_two), state)
            return (projected, columns, *state)
        finish("both")
        finish("first")
        finish("second")
        middle = half * CHUNKS[0] // sum(CHUNKS)
        both = summed["both"]
        grad = jnp.concatenate([both[:, :middle], summed["first"], both[:, middle:], summed["second"]], axis=1)
        grad = reordered(grad, order_of_rows, subs).astype(jnp.float32)
        updated = adamw(master, moment_one, moment_two, grad)
        return (projected, columns, *updated)

    return body


def power_of_two(n):
    return n > 0 and n & (n - 1) == 0


def solution(mesh):
    groups, shards = mesh.shape["grp"], mesh.shape["shard"]
    regular = power_of_two(groups) and power_of_two(shards) and groups >= 2 and shards >= 8
    token, state = P(("grp", "shard"), None), P("shard", None)
    return jax.shard_map(
        make_body(groups, shards) if regular else plain_body,
        mesh=mesh,
        in_specs=(token, token, state, state, state),
        out_specs=(token, token, state, state, state),
        check_vma=False,
    )
```

```python
import jax
import jax.numpy as jnp
from jax import lax
from jax.experimental import pallas as pl
from jax.experimental.pallas import tpu as pltpu
from jax.sharding import PartitionSpec as P

first_fix = 0.99997343860111
second_fix = 0.99407947078
CHUNKS = (5, 3)


def adamw(master, moment_one, moment_two, grad):
    one_new = 0.9 * moment_one + 0.1 * grad
    two_new = 0.95 * moment_two + 0.05 * grad * grad
    update = one_new / first_fix / (jnp.sqrt(two_new / second_fix) + 1e-08)
    master_new = master - 0.01 * (update + 0.1 * master)
    return (master_new, one_new, two_new)


def plain_body(context, cotangent, master, moment_one, moment_two):
    weights = lax.all_gather(master.astype(jnp.bfloat16), "shard", axis=0, tiled=True)
    projected = jnp.dot(context, weights, preferred_element_type=jnp.float32).astype(jnp.bfloat16)
    context_grad = lax.dot_general(
        cotangent, weights, (((1,), (1,)), ((), ())), preferred_element_type=jnp.float32
    ).astype(jnp.bfloat16)
    partial_grad = lax.psum_scatter(
        lax.dot_general(
            context, cotangent, (((0,), (0,)), ((), ())), preferred_element_type=jnp.float32
        ).astype(jnp.bfloat16),
        "shard",
        scatter_dimension=0,
        tiled=True,
    )
    grad = lax.psum(partial_grad, "grp").astype(jnp.float32)
    return (projected, context_grad, *adamw(master, moment_one, moment_two, grad))


ANY = pl.BlockSpec(memory_space=pl.ANY)
SMEM = pl.BlockSpec(memory_space=pltpu.SMEM)
VMEM = pl.BlockSpec(memory_space=pltpu.VMEM)


def dot(a, b, contract=(1, 0)):
    return lax.dot_general(a, b, (((contract[0],), (contract[1],)), ((), ())), preferred_element_type=jnp.float32)


def after(array, *others):
    return lax.optimization_barrier((array, *others))[0]


def add(a, b):
    return (a.astype(jnp.float32) + b.astype(jnp.float32)).astype(jnp.bfloat16)


def call(kernel, name, flops, outs, in_specs, out_specs, scratch=(), aliases=None):
    return pl.pallas_call(
        kernel,
        out_shape=outs,
        in_specs=in_specs,
        out_specs=out_specs,
        scratch_shapes=list(scratch),
        input_output_aliases=aliases or {},
        compiler_params=pltpu.CompilerParams(vmem_limit_bytes=24 * 2**20),
        cost_estimate=pl.CostEstimate(flops=16 * flops, bytes_accessed=0, transcendentals=0),
        name=name,
    )


def aligned(index, rows):
    return pl.ds(pl.multiple_of(index * rows, rows), rows)


def grad_blocks(info, parts, contexts, cotangents, rows, subs):
    tokens, width = cotangents[0].shape
    half = width // 2
    sizes = [half * units // sum(CHUNKS) for units in CHUNKS]
    starts = [sum(sizes[:k]) for k in range(len(sizes))]
    count = len(parts[0])
    order = sorted({r for part in parts for r in part}, key=lambda r: -sum(r in part for part in parts))
    step = rows // subs

    def spans(r):
        wanted = [h for h in range(2) if r in parts[h]]
        return wanted[0] * half, (wanted[-1] + 1) * half

    def fill(info_ref, c0, c1, t0, t1, *out_refs):
        for r in order:
            at = aligned(info_ref[0] ^ r, rows)
            lo, hi = spans(r)
            total = dot(c0[:, at], t0[:, lo:hi], (0, 0)) + dot(c1[:, at], t1[:, lo:hi], (0, 0))
            total = total.astype(jnp.bfloat16)
            for h in range(2):
                if r in parts[h]:
                    for k, size in enumerate(sizes):
                        start = h * half + starts[k] - lo
                        for j in range(subs):
                            place = pl.multiple_of(parts[h].index(r) * rows + (info_ref[1] ^ j) * step, step)
                            out_refs[2 * k + h][pl.ds(place, step), :] = total[j * step : (j + 1) * step, start : start + size]

    def plain(h, k):
        cols = slice(h * half + starts[k], h * half + starts[k] + sizes[k])
        result = []
        for r in parts[h]:
            total = sum(
                dot(lax.dynamic_slice_in_dim(c, (info[0] ^ r) * rows, rows, axis=1), t[:, cols], (0, 0))
                for c, t in zip(contexts, cotangents)
            )
            result.append(reordered(total.astype(jnp.bfloat16), info[1], subs))
        return jnp.concatenate(result, axis=0)

    if rows % 128 or step % 16:
        return [[plain(h, k) for h in range(2)] for k in range(len(sizes))]
    outs = tuple(jax.ShapeDtypeStruct((count * rows, size), jnp.bfloat16) for size in sizes for _ in range(2))
    flops = 4 * count * rows * width * tokens
    result = call(fill, "grad_blocks", flops, outs, [SMEM] + [VMEM] * 4, (VMEM,) * len(outs))(info, *contexts, *cotangents)
    return [[result[2 * k + h] for h in range(2)] for k in range(len(sizes))]


def reordered(array, low, subs):
    step = array.shape[0] // subs
    return jnp.concatenate(
        [lax.dynamic_slice_in_dim(array, (low ^ j) * step, step, axis=0) for j in range(subs)], axis=0
    )


def sources(pieces):
    arrays = []
    for piece in pieces:
        if not any(piece[2] is array for array in arrays):
            arrays.append(piece[2])
    return arrays, [[piece[2] is array for array in arrays].index(True) for piece in pieces]


def started(pairs, sems, first=0):
    copies = [pltpu.make_async_copy(a, b, sems.at[first + i]) for i, (a, b) in enumerate(pairs)]
    for copy in copies:
        copy.start()
    return copies


def wait(copies):
    for copy in copies:
        copy.wait()


def weight_copies(info_ref, pieces, index, refs, blocks, weights, rows, half):
    size = weights.shape[1] // 2
    lo = pl.multiple_of((lax.rem(info_ref[1], 2) ^ half) * size, size)
    copies = {}
    for (r, which, _, row), source in zip(pieces, index):
        if which in (None, half):
            origin = refs[source].at[pl.ds(row, rows), :]
            if which is None:
                origin = refs[source].at[pl.ds(row, rows), pl.ds(lo, size)]
            copies[r] = (origin, weights.at[pl.ds(blocks.index(r) * rows, rows), pl.ds(half * size, size)])
    return copies


def product(info, pieces, context, rows, got=None):
    tokens, width = context.shape
    half = width // 2
    blocks = sorted({piece[0] for piece in pieces})
    depth = len(blocks) * rows
    arrays, index = sources(pieces)
    more = [] if got is None else [got]
    tile = min(512, half)
    tiles = half // tile
    reads = len(blocks)

    def kernel(info_ref, context_ref, *rest):
        refs = rest[: len(arrays)]
        got_refs = rest[len(arrays) : len(arrays) + len(more)]
        out_ref, weights, chosen, result, in_sems, out_sems, *held = rest[len(arrays) + len(more) :]
        columns = [
            (context_ref.at[:, aligned(info_ref[0] ^ r, rows)], chosen.at[:, pl.ds(i * rows, rows)])
            for i, r in enumerate(blocks)
        ]
        inward = [started(columns, in_sems)]
        for side in range(2):
            pairs = weight_copies(info_ref, pieces, index, refs, blocks, weights, rows, side)
            inward.append(started([pairs[r] for r in blocks], in_sems, reads * (1 + side)))
        adding = started(list(zip(got_refs, held)), in_sems, 3 * reads)
        wait(inward[0])
        outward = []
        for side in range(2):
            wait(inward[1 + side])
            lo = (lax.rem(info_ref[1], 2) ^ side) * half
            for i in range(tiles):
                part = dot(chosen[...], weights[:, pl.ds(side * half + i * tile, tile)])
                at = pl.ds(pl.multiple_of(lo + i * tile, tile), tile)
                if more:
                    wait(adding)
                    adding = []
                    part = part + held[0][:, at].astype(jnp.float32)
                place = side * tiles + i
                result[:, pl.ds(place * tile, tile)] = part.astype(jnp.bfloat16)
                outward += started([(result.at[:, pl.ds(place * tile, tile)], out_ref.at[:, at])], out_sems, place)
        wait(outward)

    return call(
        kernel,
        "product",
        0 if more else 2 * tokens * depth * width,
        jax.ShapeDtypeStruct((tokens, width), jnp.bfloat16),
        [SMEM, ANY] + [ANY] * (len(arrays) + len(more)),
        ANY,
        [
            pltpu.VMEM((depth, width), jnp.bfloat16),
            pltpu.VMEM((tokens, depth), jnp.bfloat16),
            pltpu.VMEM((tokens, width), jnp.bfloat16),
            pltpu.SemaphoreType.DMA((3 * reads + 1,)),
            pltpu.SemaphoreType.DMA((2 * tiles,)),
        ]
        + [pltpu.VMEM((tokens, width), jnp.bfloat16)] * len(more),
    )(info, context, *arrays, *more)


def grad_columns(info, pieces, cotangent, rows, got=None):
    tokens, width = cotangent.shape
    half = width // 2
    blocks = sorted({piece[0] for piece in pieces})
    depth = len(blocks) * rows
    arrays, index = sources(pieces)
    more = [] if got is None else [got]
    reads = len(blocks)
    group = max(1, reads // 2)

    def kernel(info_ref, cotangent_ref, *rest):
        refs = rest[: len(arrays)]
        got_refs = rest[len(arrays) : len(arrays) + len(more)]
        out_ref, weights, turned, result, in_sems, out_sems, *held = rest[len(arrays) + len(more) :]
        halves = []
        for side in range(2):
            lo = pl.multiple_of((lax.rem(info_ref[1], 2) ^ side) * half, half)
            halves.append((cotangent_ref.at[:, pl.ds(lo, half)], turned.at[:, pl.ds(side * half, half)]))
        first = started(halves, in_sems, 2 * reads)
        pairs = [weight_copies(info_ref, pieces, index, refs, blocks, weights, rows, side) for side in range(2)]
        inward = [started([pairs[side][r] for side in range(2)], in_sems, 2 * i) for i, r in enumerate(blocks)]
        placing = started(list(zip(got_refs, held)), in_sems, 2 * reads + 2)
        outward = []
        wait(first)
        for start in range(0, reads, group):
            for i in range(start, start + group):
                wait(inward[i])
            at = pl.ds(start * rows, group * rows)
            result[:, at] = dot(turned[...], weights[at, :], (1, 1)).astype(jnp.bfloat16)
            for i in range(start, start + group):
                at = pl.ds(i * rows, rows)
                target = out_ref.at[:, aligned(info_ref[0] ^ blocks[i], rows) if more else at]
                outward += started([(result.at[:, at], target)], out_sems, i)
            if placing:
                wait(placing)
                placing = []
                for i, r in enumerate(blocks):
                    target = out_ref.at[:, aligned(info_ref[0] ^ r ^ 1, rows)]
                    outward += started([(held[0].at[:, pl.ds(i * rows, rows)], target)], out_sems, reads + i)
        wait(outward)

    return call(
        kernel,
        "grad_columns",
        2 * tokens * depth * width,
        jax.ShapeDtypeStruct((tokens, width if more else depth), jnp.bfloat16),
        [SMEM, ANY] + [ANY] * (len(arrays) + len(more)),
        ANY,
        [
            pltpu.VMEM((depth, width), jnp.bfloat16),
            pltpu.VMEM((tokens, width), jnp.bfloat16),
            pltpu.VMEM((tokens, depth), jnp.bfloat16),
            pltpu.SemaphoreType.DMA((2 * reads + 3,)),
            pltpu.SemaphoreType.DMA((2 * reads,)),
        ]
        + [pltpu.VMEM((tokens, depth), jnp.bfloat16)] * len(more),
    )(info, cotangent, *arrays, *more)


def stepped(info, side, pieces, state, so_far=None):
    rows, width = state[0].shape
    lines = rows // 2
    arrays = []
    for piece in pieces:
        if not any(piece[0] is array for array in arrays):
            arrays.append(piece[0])
    more = [] if so_far is None else list(so_far)

    def kernel(info_ref, *rest):
        grads, rest = rest[: len(arrays)], rest[len(arrays) :]
        states, rest = rest[:3], rest[3 + len(more) :]
        outs, held, results, in_sems, out_sems = rest[:3], rest[3:6], rest[6:9], rest[9], rest[10]
        at = aligned(info_ref[1] ^ side, lines)
        inward, outward = [], []
        for n, (_, _, to, size) in enumerate(pieces):
            cols = pl.ds(to, size)
            inward.append(started([(states[i].at[at, cols], held[i].at[:, cols]) for i in range(3)], in_sems, 3 * n))
        for n, (array, start, to, size) in enumerate(pieces):
            wait(inward[n])
            cols = pl.ds(to, size)
            grad_ref = grads[[array is other for other in arrays].index(True)]
            grad = grad_ref[:, pl.ds(start, size)].astype(jnp.float32)
            values = adamw(held[0][:, cols], held[1][:, cols], held[2][:, cols], grad)
            for result, value in zip(results, values):
                result[:, cols] = value
            outward += started([(results[i].at[:, cols], outs[i].at[at, cols]) for i in range(3)], out_sems, 3 * n)
        wait(outward)

    out = jax.ShapeDtypeStruct((rows, width), jnp.float32)
    first = 4 + len(arrays)
    return call(
        kernel,
        "stepped",
        512 * lines * width if so_far is None else 0,
        (out,) * 3,
        [SMEM] + [VMEM] * len(arrays) + [ANY] * (3 + len(more)),
        (ANY,) * 3,
        [pltpu.VMEM((lines, width), jnp.float32)] * 6 + [pltpu.SemaphoreType.DMA((3 * len(pieces),))] * 2,
        {first + i: i for i in range(3)} if more else {},
    )(info, *arrays, *state, *more)


def plain_products(info, pieces, context, cotangent, rows):
    width = context.shape[1]
    weights = jnp.zeros((width, width), jnp.bfloat16)
    for r, half, array, row in pieces:
        lo = 0 if half is None else (lax.rem(info[1], 2) ^ half) * (width // 2)
        weights = lax.dynamic_update_slice(weights, array[row : row + rows], ((info[0] ^ r) * rows, lo))
    return dot(context, weights).astype(jnp.bfloat16), dot(cotangent, weights, (1, 1)).astype(jnp.bfloat16)


def make_body(groups, shards):
    bits = shards.bit_length() - 1
    x_masks = [2 << i for i in range((bits - 1) // 2)]
    y_masks = [2 << i for i in range((bits - 1) // 2, bits - 1)]
    masks = (x_masks + y_masks, y_masks + x_masks)
    subs = groups // 2
    group_masks = [1 << i for i in reversed(range(subs.bit_length() - 1))]

    def swap(array, mask):
        return lax.ppermute(array, "shard", [(i, i ^ mask) for i in range(shards)])

    def swap_group(array, mask):
        return lax.ppermute(array, "grp", [(i, i ^ mask) for i in range(groups)])

    def spread(pieces, masks):
        for mask in masks:
            pieces = {**pieces, **{r ^ mask: swap(piece, mask) for r, piece in pieces.items()}}
        return pieces

    def halving(masks):
        blocks = [0]
        for mask in reversed(masks):
            blocks = blocks + [b ^ mask for b in blocks]
        return blocks

    def body(context, cotangent, master, moment_one, moment_two):
        shard, group = lax.axis_index("shard"), lax.axis_index("grp")
        rows, width = master.shape
        half = width // 2
        odd = lax.rem(group, 2)
        low = lax.rem(group, subs)
        info = jnp.stack([shard, low if subs > 1 else odd])
        order_of_rows = low
        tiled = rows % 128 == 0 and subs == 2
        latest = []

        def then(array):
            return after(array, *latest)

        def did(result):
            latest[:] = [result]
            return result

        def named(names, array, flip=0):
            return [(r, h ^ flip, array, i * rows) for i, (r, h) in enumerate(names)]

        contexts, cotangents = (context, swap(context, 1)), (cotangent, swap(cotangent, 1))

        left, right = master[:, :half], master[:, half:]
        mine, other = jnp.where(odd == 1, right, left), jnp.where(odd == 1, left, right)
        mine, other = mine.astype(jnp.bfloat16), other.astype(jnp.bfloat16)
        near_x = {r: p for r, p in spread({0: mine}, x_masks).items() if r}
        near_y = {r: p for r, p in spread({0: other}, y_masks).items() if r}

        chunk_sizes = [half * units // sum(CHUNKS) for units in CHUNKS]
        orders = [halving(m) for m in masks]
        count = len(orders[0]) // 2
        sent = grad_blocks(info, [o[count:] for o in orders], contexts, cotangents, rows, subs)
        did(sent[-1][-1])
        got = {0: [swap(sent[0][h], masks[h][0]) for h in range(2)]}

        kept = grad_blocks(info, [o[:count] for o in orders], contexts, (then(cotangent), cotangents[1]), rows, subs)
        did(kept[-1][-1])

        far_x = spread({r: then(p) for r, p in near_x.items()}, y_masks)
        far_y = spread({r: then(p) for r, p in near_y.items()}, x_masks)
        far_names = [(r, 0) for r in far_x if r not in near_x] + [(r, 1) for r in far_y if r not in near_y]
        far = [(far_x, far_y)[h][r] for r, h in far_names]
        near = jnp.concatenate([then(p) for p in [*near_x.values(), *near_y.values()]], axis=0)
        near_names = [(r, 0) for r in near_x] + [(r, 1) for r in near_y]
        near_group = swap_group(near, 1)
        weights = then(master).astype(jnp.bfloat16)
        pieces = [(0, None, weights, 0)] + named(near_names, near) + named(near_names, near_group, flip=1)
        pieces += [(r, h, array, 0) for (r, h), array in zip(far_names, far)]
        def halve_all(k, level):
            come, got[k] = got[k], [None, None]
            for h in range(2):
                total = did(add(kept[k][h], then(come[h])))
                size = total.shape[0] // 2
                kept[k][h], got[k][h] = total[:size], swap(total[size:], masks[h][level])

        summed, come, stage = {}, {}, {}

        def enter(k, name, halves):
            parts = [did(add(kept[k][h], then(got[k][h]))) for h in halves]
            summed[name], stage[name] = jnp.concatenate(parts, axis=1) if len(parts) > 1 else parts[0], 0
            leave(name)

        def leave(k):
            j, steps = stage[k], len(group_masks)
            if j < steps:
                size = summed[k].shape[0] // 2
                come[k] = swap_group(summed[k][size:], group_masks[j])
                summed[k] = summed[k][:size]
            elif j == steps:
                come[k] = swap_group(summed[k], subs)
            elif j <= 2 * steps:
                come[k] = swap_group(summed[k], group_masks[2 * steps - j])

        def advance(k):
            if stage[k] <= len(group_masks):
                summed[k] = did(add(summed[k], then(come[k])))
            else:
                summed[k] = jnp.concatenate([summed[k], then(come[k])], axis=0)
            stage[k] += 1
            leave(k)

        last = 2 * len(group_masks) + 1
        levels = len(masks[0])

        def halve_to_end(k, start):
            for level in range(start, levels):
                halve_all(k, level)

        def finish(name):
            while stage[name] < last:
                advance(name)

        halve_to_end(0, 1)
        got[1] = [swap(after(sent[1][h], *latest, *far), masks[h][0]) for h in range(2)]
        enter(0, "first", (0, 1))
        if tiled:
            part = did(product(info, pieces, then(contexts[1]), rows))
            got_part = swap(part, 1)
        halve_to_end(1, 1)
        advance("first")
        if tiled:
            columns = did(grad_columns(info, pieces, then(cotangents[1]), rows))
            got_columns = swap(columns, 1)
        enter(1, "rest", (0, 1))
        if tiled:
            projected = did(product(info, pieces, then(context), rows, got_part))
        else:
            pieces += [(r ^ 1, h, swap(array, 1), row) for r, h, array, row in pieces]
            projected, columns = plain_products(info, pieces, context, cotangent, rows)
        advance("first")
        advance("rest")
        if tiled:
            sizes = chunk_sizes

            def columns_of(array, k):
                start = k * sizes[0]
                return [(array, 0, start, sizes[k]), (array, sizes[k], half + start, sizes[k])]

            state = (master, moment_one, moment_two)
            so_far = stepped(info, 0, columns_of(summed["first"], 0), (then(master), *state[1:]))
            did(so_far[0])
            columns = did(grad_columns(info, pieces, then(cotangent), rows, got_columns))
        advance("rest")
        if tiled:
            so_far = stepped(info, 0, columns_of(summed["rest"], 1), state, so_far)
            grads = columns_of(come["first"], 0) + columns_of(come["rest"], 1)
            return (projected, columns, *stepped(info, 1, grads, state, so_far))
        finish("first")
        finish("rest")
        named_sizes = list(zip(("first", "rest"), chunk_sizes))
        parts = [summed[name][:, h * size : (h + 1) * size] for h in range(2) for name, size in named_sizes]
        grad = jnp.concatenate(parts, axis=1)
        grad = reordered(grad, order_of_rows, subs).astype(jnp.float32)
        updated = adamw(master, moment_one, moment_two, grad)
        return (projected, columns, *updated)

    return body


def power_of_two(n):
    return n > 0 and n & (n - 1) == 0


def solution(mesh):
    groups, shards = mesh.shape["grp"], mesh.shape["shard"]
    regular = power_of_two(groups) and power_of_two(shards) and groups >= 2 and shards >= 8
    token, state = P(("grp", "shard"), None), P("shard", None)
    return jax.shard_map(
        make_body(groups, shards) if regular else plain_body,
        mesh=mesh,
        in_specs=(token, token, state, state, state),
        out_specs=(token, token, state, state, state),
        check_vma=False,
    )
```

```python
import jax
import jax.numpy as jnp
from jax import lax
from jax.experimental import pallas as pl
from jax.experimental.pallas import tpu as pltpu
from jax.sharding import PartitionSpec as P

first_fix = 0.99997343860111
second_fix = 0.99407947078
CHUNKS = (5, 3)


def adamw(master, moment_one, moment_two, grad):
    one_new = 0.9 * moment_one + 0.1 * grad
    two_new = 0.95 * moment_two + 0.05 * grad * grad
    update = one_new / first_fix / (jnp.sqrt(two_new / second_fix) + 1e-08)
    master_new = master - 0.01 * (update + 0.1 * master)
    return (master_new, one_new, two_new)


def plain_body(context, cotangent, master, moment_one, moment_two):
    weights = lax.all_gather(master.astype(jnp.bfloat16), "shard", axis=0, tiled=True)
    projected = jnp.dot(context, weights, preferred_element_type=jnp.float32).astype(jnp.bfloat16)
    context_grad = lax.dot_general(
        cotangent, weights, (((1,), (1,)), ((), ())), preferred_element_type=jnp.float32
    ).astype(jnp.bfloat16)
    partial_grad = lax.psum_scatter(
        lax.dot_general(
            context, cotangent, (((0,), (0,)), ((), ())), preferred_element_type=jnp.float32
        ).astype(jnp.bfloat16),
        "shard",
        scatter_dimension=0,
        tiled=True,
    )
    grad = lax.psum(partial_grad, "grp").astype(jnp.float32)
    return (projected, context_grad, *adamw(master, moment_one, moment_two, grad))


ANY = pl.BlockSpec(memory_space=pl.ANY)
SMEM = pl.BlockSpec(memory_space=pltpu.SMEM)
VMEM = pl.BlockSpec(memory_space=pltpu.VMEM)


def dot(a, b, contract=(1, 0)):
    return lax.dot_general(a, b, (((contract[0],), (contract[1],)), ((), ())), preferred_element_type=jnp.float32)


def after(array, *others):
    return lax.optimization_barrier((array, *others))[0]


def add(a, b):
    return (a.astype(jnp.float32) + b.astype(jnp.float32)).astype(jnp.bfloat16)


def call(kernel, name, flops, outs, in_specs, out_specs, scratch=(), aliases=None):
    return pl.pallas_call(
        kernel,
        out_shape=outs,
        in_specs=in_specs,
        out_specs=out_specs,
        scratch_shapes=list(scratch),
        input_output_aliases=aliases or {},
        compiler_params=pltpu.CompilerParams(vmem_limit_bytes=24 * 2**20),
        cost_estimate=pl.CostEstimate(flops=16 * flops, bytes_accessed=0, transcendentals=0),
        name=name,
    )


def aligned(index, rows):
    return pl.ds(pl.multiple_of(index * rows, rows), rows)


def grad_blocks(info, parts, contexts, cotangents, rows, subs):
    tokens, width = cotangents[0].shape
    half = width // 2
    sizes = [half * units // sum(CHUNKS) for units in CHUNKS]
    starts = [sum(sizes[:k]) for k in range(len(sizes))]
    count = len(parts[0])
    order = sorted({r for part in parts for r in part}, key=lambda r: -sum(r in part for part in parts))
    step = rows // subs

    def spans(r):
        wanted = [h for h in range(2) if r in parts[h]]
        return wanted[0] * half, (wanted[-1] + 1) * half

    def fill(info_ref, c0, c1, t0, t1, *out_refs):
        for r in order:
            at = aligned(info_ref[0] ^ r, rows)
            lo, hi = spans(r)
            total = dot(c0[:, at], t0[:, lo:hi], (0, 0)) + dot(c1[:, at], t1[:, lo:hi], (0, 0))
            total = total.astype(jnp.bfloat16)
            for h in range(2):
                if r in parts[h]:
                    for k, size in enumerate(sizes):
                        start = h * half + starts[k] - lo
                        for j in range(subs):
                            place = pl.multiple_of(parts[h].index(r) * rows + (info_ref[1] ^ j) * step, step)
                            out_refs[2 * k + h][pl.ds(place, step), :] = total[j * step : (j + 1) * step, start : start + size]

    def plain(h, k):
        cols = slice(h * half + starts[k], h * half + starts[k] + sizes[k])
        result = []
        for r in parts[h]:
            total = sum(
                dot(lax.dynamic_slice_in_dim(c, (info[0] ^ r) * rows, rows, axis=1), t[:, cols], (0, 0))
                for c, t in zip(contexts, cotangents)
            )
            result.append(reordered(total.astype(jnp.bfloat16), info[1], subs))
        return jnp.concatenate(result, axis=0)

    if rows % 128 or step % 16:
        return [[plain(h, k) for h in range(2)] for k in range(len(sizes))]
    outs = tuple(jax.ShapeDtypeStruct((count * rows, size), jnp.bfloat16) for size in sizes for _ in range(2))
    flops = 4 * count * rows * width * tokens
    result = call(fill, "grad_blocks", flops, outs, [SMEM] + [VMEM] * 4, (VMEM,) * len(outs))(info, *contexts, *cotangents)
    return [[result[2 * k + h] for h in range(2)] for k in range(len(sizes))]


def reordered(array, low, subs):
    step = array.shape[0] // subs
    return jnp.concatenate(
        [lax.dynamic_slice_in_dim(array, (low ^ j) * step, step, axis=0) for j in range(subs)], axis=0
    )


def sources(pieces):
    arrays = []
    for piece in pieces:
        if not any(piece[2] is array for array in arrays):
            arrays.append(piece[2])
    return arrays, [[piece[2] is array for array in arrays].index(True) for piece in pieces]


def started(pairs, sems, first=0):
    copies = [pltpu.make_async_copy(a, b, sems.at[first + i]) for i, (a, b) in enumerate(pairs)]
    for copy in copies:
        copy.start()
    return copies


def wait(copies):
    for copy in copies:
        copy.wait()


def weight_copies(info_ref, pieces, index, refs, blocks, weights, rows, half):
    size = weights.shape[1] // 2
    lo = pl.multiple_of((lax.rem(info_ref[1], 2) ^ half) * size, size)
    copies = {}
    for (r, which, _, row), source in zip(pieces, index):
        if which in (None, half):
            origin = refs[source].at[pl.ds(row, rows), :]
            if which is None:
                origin = refs[source].at[pl.ds(row, rows), pl.ds(lo, size)]
            copies[r] = (origin, weights.at[pl.ds(blocks.index(r) * rows, rows), pl.ds(half * size, size)])
    return copies


def product(info, pieces, context, rows, got=None):
    tokens, width = context.shape
    half = width // 2
    blocks = sorted({piece[0] for piece in pieces})
    depth = len(blocks) * rows
    arrays, index = sources(pieces)
    more = [] if got is None else [got]
    tile = min(512, half)
    tiles = half // tile
    reads = len(blocks)

    def kernel(info_ref, context_ref, *rest):
        refs = rest[: len(arrays)]
        got_refs = rest[len(arrays) : len(arrays) + len(more)]
        out_ref, weights, chosen, result, in_sems, out_sems, *held = rest[len(arrays) + len(more) :]
        columns = [
            (context_ref.at[:, aligned(info_ref[0] ^ r, rows)], chosen.at[:, pl.ds(i * rows, rows)])
            for i, r in enumerate(blocks)
        ]
        inward = [started(columns, in_sems)]
        for side in range(2):
            pairs = weight_copies(info_ref, pieces, index, refs, blocks, weights, rows, side)
            inward.append(started([pairs[r] for r in blocks], in_sems, reads * (1 + side)))
        adding = started(list(zip(got_refs, held)), in_sems, 3 * reads)
        wait(inward[0])
        outward = []
        for side in range(2):
            wait(inward[1 + side])
            lo = (lax.rem(info_ref[1], 2) ^ side) * half
            for i in range(tiles):
                part = dot(chosen[...], weights[:, pl.ds(side * half + i * tile, tile)])
                at = pl.ds(pl.multiple_of(lo + i * tile, tile), tile)
                if more:
                    wait(adding)
                    adding = []
                    part = part + held[0][:, at].astype(jnp.float32)
                place = side * tiles + i
                result[:, pl.ds(place * tile, tile)] = part.astype(jnp.bfloat16)
                outward += started([(result.at[:, pl.ds(place * tile, tile)], out_ref.at[:, at])], out_sems, place)
        wait(outward)

    return call(
        kernel,
        "product",
        0 if more else 2 * tokens * depth * width,
        jax.ShapeDtypeStruct((tokens, width), jnp.bfloat16),
        [SMEM, ANY] + [ANY] * (len(arrays) + len(more)),
        ANY,
        [
            pltpu.VMEM((depth, width), jnp.bfloat16),
            pltpu.VMEM((tokens, depth), jnp.bfloat16),
            pltpu.VMEM((tokens, width), jnp.bfloat16),
            pltpu.SemaphoreType.DMA((3 * reads + 1,)),
            pltpu.SemaphoreType.DMA((2 * tiles,)),
        ]
        + [pltpu.VMEM((tokens, width), jnp.bfloat16)] * len(more),
    )(info, context, *arrays, *more)


def grad_columns(info, pieces, cotangent, rows, got=None):
    tokens, width = cotangent.shape
    half = width // 2
    blocks = sorted({piece[0] for piece in pieces})
    depth = len(blocks) * rows
    arrays, index = sources(pieces)
    more = [] if got is None else [got]
    reads = len(blocks)
    group = max(1, reads // 2)

    def kernel(info_ref, cotangent_ref, *rest):
        refs = rest[: len(arrays)]
        got_refs = rest[len(arrays) : len(arrays) + len(more)]
        out_ref, weights, turned, result, in_sems, out_sems, *held = rest[len(arrays) + len(more) :]
        halves = []
        for side in range(2):
            lo = pl.multiple_of((lax.rem(info_ref[1], 2) ^ side) * half, half)
            halves.append((cotangent_ref.at[:, pl.ds(lo, half)], turned.at[:, pl.ds(side * half, half)]))
        first = started(halves, in_sems, 2 * reads)
        pairs = [weight_copies(info_ref, pieces, index, refs, blocks, weights, rows, side) for side in range(2)]
        inward = [started([pairs[side][r] for side in range(2)], in_sems, 2 * i) for i, r in enumerate(blocks)]
        placing = started(list(zip(got_refs, held)), in_sems, 2 * reads + 2)
        outward = []
        wait(first)
        for start in range(0, reads, group):
            for i in range(start, start + group):
                wait(inward[i])
            at = pl.ds(start * rows, group * rows)
            result[:, at] = dot(turned[...], weights[at, :], (1, 1)).astype(jnp.bfloat16)
            for i in range(start, start + group):
                at = pl.ds(i * rows, rows)
                target = out_ref.at[:, aligned(info_ref[0] ^ blocks[i], rows) if more else at]
                outward += started([(result.at[:, at], target)], out_sems, i)
            if placing:
                wait(placing)
                placing = []
                for i, r in enumerate(blocks):
                    target = out_ref.at[:, aligned(info_ref[0] ^ r ^ 1, rows)]
                    outward += started([(held[0].at[:, pl.ds(i * rows, rows)], target)], out_sems, reads + i)
        wait(outward)

    return call(
        kernel,
        "grad_columns",
        2 * tokens * depth * width,
        jax.ShapeDtypeStruct((tokens, width if more else depth), jnp.bfloat16),
        [SMEM, ANY] + [ANY] * (len(arrays) + len(more)),
        ANY,
        [
            pltpu.VMEM((depth, width), jnp.bfloat16),
            pltpu.VMEM((tokens, width), jnp.bfloat16),
            pltpu.VMEM((tokens, depth), jnp.bfloat16),
            pltpu.SemaphoreType.DMA((2 * reads + 3,)),
            pltpu.SemaphoreType.DMA((2 * reads,)),
        ]
        + [pltpu.VMEM((tokens, depth), jnp.bfloat16)] * len(more),
    )(info, cotangent, *arrays, *more)


def stepped(info, side, pieces, state, so_far=None):
    rows, width = state[0].shape
    lines = rows // 2
    arrays = []
    for piece in pieces:
        if not any(piece[0] is array for array in arrays):
            arrays.append(piece[0])
    more = [] if so_far is None else list(so_far)

    def kernel(info_ref, *rest):
        grads, rest = rest[: len(arrays)], rest[len(arrays) :]
        states, rest = rest[:3], rest[3 + len(more) :]
        outs, held, results, in_sems, out_sems = rest[:3], rest[3:6], rest[6:9], rest[9], rest[10]
        at = aligned(info_ref[1] ^ side, lines)
        inward, outward = [], []
        for n, (_, _, to, size) in enumerate(pieces):
            cols = pl.ds(to, size)
            inward.append(started([(states[i].at[at, cols], held[i].at[:, cols]) for i in range(3)], in_sems, 3 * n))
        for n, (array, start, to, size) in enumerate(pieces):
            wait(inward[n])
            cols = pl.ds(to, size)
            grad_ref = grads[[array is other for other in arrays].index(True)]
            grad = grad_ref[:, pl.ds(start, size)].astype(jnp.float32)
            values = adamw(held[0][:, cols], held[1][:, cols], held[2][:, cols], grad)
            for result, value in zip(results, values):
                result[:, cols] = value
            outward += started([(results[i].at[:, cols], outs[i].at[at, cols]) for i in range(3)], out_sems, 3 * n)
        wait(outward)

    out = jax.ShapeDtypeStruct((rows, width), jnp.float32)
    first = 4 + len(arrays)
    return call(
        kernel,
        "stepped",
        512 * lines * width if so_far is None else 0,
        (out,) * 3,
        [SMEM] + [VMEM] * len(arrays) + [ANY] * (3 + len(more)),
        (ANY,) * 3,
        [pltpu.VMEM((lines, width), jnp.float32)] * 6 + [pltpu.SemaphoreType.DMA((3 * len(pieces),))] * 2,
        {first + i: i for i in range(3)} if more else {},
    )(info, *arrays, *state, *more)


def plain_products(info, pieces, context, cotangent, rows):
    width = context.shape[1]
    weights = jnp.zeros((width, width), jnp.bfloat16)
    for r, half, array, row in pieces:
        lo = 0 if half is None else (lax.rem(info[1], 2) ^ half) * (width // 2)
        weights = lax.dynamic_update_slice(weights, array[row : row + rows], ((info[0] ^ r) * rows, lo))
    return dot(context, weights).astype(jnp.bfloat16), dot(cotangent, weights, (1, 1)).astype(jnp.bfloat16)


def make_body(groups, shards):
    bits = shards.bit_length() - 1
    x_masks = [2 << i for i in range((bits - 1) // 2)]
    y_masks = [2 << i for i in range((bits - 1) // 2, bits - 1)]
    masks = (x_masks + y_masks, y_masks + x_masks)
    subs = groups // 2
    group_masks = [1 << i for i in reversed(range(subs.bit_length() - 1))]

    def swap(array, mask):
        return lax.ppermute(array, "shard", [(i, i ^ mask) for i in range(shards)])

    def swap_group(array, mask):
        return lax.ppermute(array, "grp", [(i, i ^ mask) for i in range(groups)])

    def spread(pieces, masks):
        for mask in masks:
            pieces = {**pieces, **{r ^ mask: swap(piece, mask) for r, piece in pieces.items()}}
        return pieces

    def halving(masks):
        blocks = [0]
        for mask in reversed(masks):
            blocks = blocks + [b ^ mask for b in blocks]
        return blocks

    def body(context, cotangent, master, moment_one, moment_two):
        shard, group = lax.axis_index("shard"), lax.axis_index("grp")
        rows, width = master.shape
        half = width // 2
        odd = lax.rem(group, 2)
        low = lax.rem(group, subs)
        info = jnp.stack([shard, low if subs > 1 else odd])
        order_of_rows = low
        tiled = rows % 128 == 0 and subs == 2
        latest = []

        def then(array):
            return after(array, *latest)

        def did(result):
            latest[:] = [result]
            return result

        def named(names, array, flip=0):
            return [(r, h ^ flip, array, i * rows) for i, (r, h) in enumerate(names)]

        contexts, cotangents = (context, swap(context, 1)), (cotangent, swap(cotangent, 1))

        left, right = master[:, :half], master[:, half:]
        mine, other = jnp.where(odd == 1, right, left), jnp.where(odd == 1, left, right)
        mine, other = mine.astype(jnp.bfloat16), other.astype(jnp.bfloat16)
        near_x = {r: p for r, p in spread({0: mine}, x_masks).items() if r}
        near_y = {r: p for r, p in spread({0: other}, y_masks).items() if r}

        chunk_sizes = [half * units // sum(CHUNKS) for units in CHUNKS]
        orders = [halving(m) for m in masks]
        count = len(orders[0]) // 2
        sent = grad_blocks(info, [o[count:] for o in orders], contexts, cotangents, rows, subs)
        did(sent[-1][-1])
        got = {0: [swap(sent[0][h], masks[h][0]) for h in range(2)]}

        kept = grad_blocks(info, [o[:count] for o in orders], contexts, (then(cotangent), cotangents[1]), rows, subs)
        did(kept[-1][-1])

        far_x = spread({r: then(p) for r, p in near_x.items()}, y_masks)
        far_y = spread({r: then(p) for r, p in near_y.items()}, x_masks)
        far_names = [(r, 0) for r in far_x if r not in near_x] + [(r, 1) for r in far_y if r not in near_y]
        far = [(far_x, far_y)[h][r] for r, h in far_names]
        near = jnp.concatenate([then(p) for p in [*near_x.values(), *near_y.values()]], axis=0)
        near_names = [(r, 0) for r in near_x] + [(r, 1) for r in near_y]
        near_group = swap_group(near, 1)
        weights = then(master).astype(jnp.bfloat16)
        pieces = [(0, None, weights, 0)] + named(near_names, near) + named(near_names, near_group, flip=1)
        pieces += [(r, h, array, 0) for (r, h), array in zip(far_names, far)]
        def halve_all(k, level):
            come, got[k] = got[k], [None, None]
            for h in range(2):
                total = did(add(kept[k][h], then(come[h])))
                size = total.shape[0] // 2
                kept[k][h], got[k][h] = total[:size], swap(total[size:], masks[h][level])

        summed, come, stage = {}, {}, {}

        def enter(k, name, halves):
            parts = [did(add(kept[k][h], then(got[k][h]))) for h in halves]
            summed[name], stage[name] = jnp.concatenate(parts, axis=1) if len(parts) > 1 else parts[0], 0
            leave(name)

        def leave(k):
            j, steps = stage[k], len(group_masks)
            if j < steps:
                size = summed[k].shape[0] // 2
                come[k] = swap_group(summed[k][size:], group_masks[j])
                summed[k] = summed[k][:size]
            elif j == steps:
                come[k] = swap_group(summed[k], subs)
            elif j <= 2 * steps:
                come[k] = swap_group(summed[k], group_masks[2 * steps - j])

        def advance(k):
            if stage[k] <= len(group_masks):
                summed[k] = did(add(summed[k], then(come[k])))
            else:
                summed[k] = jnp.concatenate([summed[k], then(come[k])], axis=0)
            stage[k] += 1
            leave(k)

        last = 2 * len(group_masks) + 1
        levels = len(masks[0])

        def halve_to_end(k, start):
            for level in range(start, levels):
                halve_all(k, level)

        def finish(name):
            while stage[name] < last:
                advance(name)

        halve_to_end(0, 1)
        got[1] = [swap(after(sent[1][h], *latest, *far), masks[h][0]) for h in range(2)]
        enter(0, "first", (0, 1))
        if tiled:
            part = did(product(info, pieces, then(contexts[1]), rows))
            got_part = swap(part, 1)
        halve_to_end(1, 1)
        advance("first")
        if tiled:
            columns = did(grad_columns(info, pieces, then(cotangents[1]), rows))
            got_columns = swap(columns, 1)
        enter(1, "rest", (0, 1))
        if tiled:
            projected = did(product(info, pieces, then(context), rows, got_part))
        else:
            pieces += [(r ^ 1, h, swap(array, 1), row) for r, h, array, row in pieces]
            projected, columns = plain_products(info, pieces, context, cotangent, rows)
        advance("first")
        advance("rest")
        if tiled:
            sizes = chunk_sizes

            def columns_of(array, k):
                start = k * sizes[0]
                return [(array, 0, start, sizes[k]), (array, sizes[k], half + start, sizes[k])]

            state = (master, moment_one, moment_two)
            so_far = stepped(info, 0, columns_of(summed["first"], 0), (then(master), *state[1:]))
            did(so_far[0])
            columns = did(grad_columns(info, pieces, then(cotangent), rows, got_columns))
        advance("rest")
        if tiled:
            so_far = stepped(info, 0, columns_of(summed["rest"], 1), state, so_far)
            so_far = stepped(info, 1, columns_of(come["first"], 0), state, so_far)
            return (projected, columns, *stepped(info, 1, columns_of(come["rest"], 1), state, so_far))
        finish("first")
        finish("rest")
        named_sizes = list(zip(("first", "rest"), chunk_sizes))
        parts = [summed[name][:, h * size : (h + 1) * size] for h in range(2) for name, size in named_sizes]
        grad = jnp.concatenate(parts, axis=1)
        grad = reordered(grad, order_of_rows, subs).astype(jnp.float32)
        updated = adamw(master, moment_one, moment_two, grad)
        return (projected, columns, *updated)

    return body


def power_of_two(n):
    return n > 0 and n & (n - 1) == 0


def solution(mesh):
    groups, shards = mesh.shape["grp"], mesh.shape["shard"]
    regular = power_of_two(groups) and power_of_two(shards) and groups >= 2 and shards >= 8
    token, state = P(("grp", "shard"), None), P("shard", None)
    return jax.shard_map(
        make_body(groups, shards) if regular else plain_body,
        mesh=mesh,
        in_specs=(token, token, state, state, state),
        out_specs=(token, token, state, state, state),
        check_vma=False,
    )
```
